32 devices in a mesh: seg: 2 (over x), smp: 8 (over z, y), snp: 2 (over core).
Axes of the slice: x: 2, y: 2, z: 4, core: 2. Of those that a mesh axis runs over, the one named last changes fastest.
Arguments:
- dosage: bfloat16 [4096, 8192], P('smp', ('seg', 'snp')), parts along dimension 1, may hold values from -48 to 48, as said below
Outputs:
- band_corr: float32 [3, 16, 512, 512], P(None, ('seg', 'snp'), 'smp'), parts along dimension 1
The draws below stay inside these ranges and needn't reach their ends.
There are 2 independent parts, one for each index of `seg`. The reference program is written for one: setup_inputs(seed, part) draws one part's arguments, and reference() takes and returns one part's arrays. A program takes and returns all parts, laid end to end along the dimension named above; each array names one. Nothing has to cross between parts.
Inputs may be any that keep to these rules, and one draw needn't show every extreme that they name: `dosage`: dosages of each SNP share part of their variation with SNPs nearby.
All inputs are finite; a program needn't handle non-finite values.
Results may differ from the reference program's by a relative error of at most 0.0003.
Values may be sent and summed in bfloat16 or wider, within the bound.
A program may use at most 128 MiB of HBM per device.

```python
import jax
import jax.numpy as jnp
from jax import lax

BLK = 512
NBLK = 8
SNPS = 4096
SAMPLES = 4096


def draw_dosage(key, part):
    key_noise, key_factor, key_load, key_scale = jax.random.split(key, 4)
    factor_count = SNPS // 64
    noise = jax.random.normal(key_noise, (SAMPLES, SNPS), jnp.float32)
    col_scale = jax.random.uniform(key_scale, (SNPS,), jnp.float32, 0.5, 2.0)
    factors = jax.random.normal(key_factor, (SAMPLES, factor_count), jnp.float32)
    columns = jnp.arange(SNPS, dtype=jnp.float32)
    centers = 64.0 * jnp.arange(factor_count, dtype=jnp.float32) + 32.0
    nearby = (jnp.abs(columns[None, :] - centers[:, None]) < 640.0).astype(jnp.float32)
    loading = jax.random.uniform(key_load, (factor_count, SNPS), jnp.float32, -0.6, 0.6) * nearby
    mixed = noise + jnp.dot(factors, loading, precision=lax.Precision.HIGHEST)
    row_scale = 0.6 + 1.2 * jnp.arange(SAMPLES, dtype=jnp.float32) / SAMPLES
    return jnp.clip(mixed * row_scale[:, None] * col_scale[None, :], -48.0, 48.0).astype(jnp.bfloat16)


def setup_inputs(seed: int = 0, part: int = 0) -> dict:
    arg_keys = jax.random.split(jax.random.key(seed), 2)
    own_keys = jax.random.split(jax.random.fold_in(arg_keys[1], part), 2)
    dosage = draw_dosage(jax.random.fold_in(jax.random.fold_in(arg_keys[1], part), 71), part)
    return {"dosage": dosage}


epsilon = 1e-06

def reference(dosage):
    squares = lax.optimization_barrier(jnp.sum(jnp.square(dosage.astype(jnp.float32)), axis=0))
    padded = jnp.pad(dosage, ((0, 0), (0, 2 * BLK)))
    squares_pad = jnp.pad(squares, (0, 2 * BLK))

    def one_block(block):
        begin = (block * BLK).astype(jnp.int32)
        left_part = lax.dynamic_slice_in_dim(dosage, begin, BLK, 1).astype(jnp.float32)
        right_part = lax.dynamic_slice_in_dim(padded, begin, 3 * BLK, 1).astype(jnp.float32)
        gram = jnp.dot(left_part.T, right_part, precision=lax.Precision.HIGHEST, preferred_element_type=jnp.float32)
        row_scale = lax.rsqrt(lax.dynamic_slice_in_dim(squares, begin, BLK, 0) + epsilon)
        col_scale = lax.rsqrt(lax.dynamic_slice_in_dim(squares_pad, begin, 3 * BLK, 0) + epsilon)
        scaled = gram * row_scale[:, None] * col_scale[None, :]
        return scaled.reshape(BLK, 3, BLK).transpose(1, 0, 2)
    stacked = lax.map(one_block, jnp.arange(NBLK, dtype=jnp.int32))
    return stacked.transpose(1, 0, 2, 3)
```

```python
import functools

import jax
import jax.numpy as jnp
from jax import lax
from jax.experimental import pallas as pl
from jax.experimental.pallas import tpu as pltpu
from jax.sharding import PartitionSpec as P

BLK = 512
EPS = 1e-06
WIRE = jnp.float32
UNIT = 1.0
LAG = 3


def kernel(n, snps, x_ref, out_ref, full, squares_all, scale, row_scale, acc, level_send, level_recv,
           far_send, far_recv, next_squares, local_sem, raw_ss, raw_rs, core_ss, core_rs, fwd_ss, fwd_rs,
           sq_ss, sq_rs, nsq_ss, nsq_rs, lev_ss, lev_rs, far_ss, far_rs):
    samples, cols = x_ref.shape
    blocks = cols // BLK
    quarter = BLK // 4
    me = lax.axis_index("smp")
    core = lax.axis_index("snp")
    has_next = core < snps - 1
    has_prev = core > 0
    near_bit, far_bit = n // 4, n // 2
    near = (me // near_bit) % 2
    far = me // far_bit
    near_peer = me + near_bit * (1 - 2 * near)
    far_peer = me + far_bit * (1 - 2 * far)
    bits = []
    bit = n // 8
    while bit >= 1:
        bits.append(bit)
        bit //= 2
    tiles = 3 * blocks

    barrier = pltpu.get_barrier_semaphore()

    @pl.loop(1, n)
    def _(d):
        pl.semaphore_signal(barrier, inc=1, device_id={"smp": lax.rem(me + d, n)})

    @pl.when(has_next)
    def _():
        pl.semaphore_signal(barrier, inc=1, device_id={"snp": core + 1})

    @pl.when(has_prev)
    def _():
        pl.semaphore_signal(barrier, inc=1, device_id={"snp": core - 1})

    load = pltpu.make_async_copy(x_ref, full.at[pl.ds(0, samples), pl.ds(0, cols)], local_sem)
    load.start()
    pl.semaphore_wait(barrier, n - 1 + jnp.where(has_next, 1, 0) + jnp.where(has_prev, 1, 0))

    def raw(b):
        return pltpu.make_async_remote_copy(
            x_ref.at[:, pl.ds(b * BLK, BLK)],
            full.at[pl.ds(samples, samples), pl.ds(b * BLK, BLK)],
            raw_ss.at[b], raw_rs.at[b], device_id={"smp": near_peer})

    def to_core():
        return pltpu.make_async_remote_copy(
            x_ref.at[:, pl.ds(0, 2 * BLK)],
            full.at[pl.ds(0, samples), pl.ds(cols, 2 * BLK)],
            core_ss, core_rs, device_id={"snp": lax.rem(core + snps - 1, snps)})

    def forward(b):
        return pltpu.make_async_remote_copy(
            full.at[pl.ds(samples, samples), pl.ds(pl.multiple_of(b * BLK, BLK), BLK)],
            full.at[pl.ds(samples, samples), pl.ds(pl.multiple_of(cols + b * BLK, BLK), BLK)],
            fwd_ss.at[b], fwd_rs.at[b], device_id={"snp": lax.rem(core + snps - 1, snps)})

    for b in range(blocks):
        raw(b).start()

    @pl.when(has_prev)
    def _():
        to_core().start()

    load.wait()
    for b in range(blocks):
        def add(r, total, b=b):
            piece = full[pl.ds(pl.multiple_of(r * 16, 16), 16), b * BLK:(b + 1) * BLK].astype(jnp.float32)
            return total + piece * piece
        total = lax.fori_loop(0, samples // 16, add, jnp.zeros((16, BLK), jnp.float32))
        squares_all[me, :, b * BLK:(b + 1) * BLK] = jnp.sum(total, axis=0, keepdims=True)

    def send_squares(d):
        peer = lax.rem(me + d, n)
        return pltpu.make_async_remote_copy(
            squares_all.at[me], squares_all.at[me], sq_ss.at[peer], sq_rs.at[me], device_id={"smp": peer})

    def recv_squares(d):
        peer = lax.rem(me + d, n)
        return pltpu.make_async_remote_copy(
            squares_all.at[peer], squares_all.at[peer], sq_ss.at[peer], sq_rs.at[peer], device_id={"smp": peer})

    @pl.loop(1, n)
    def _(d):
        send_squares(d).start()

    @pl.loop(1, n)
    def _(d):
        recv_squares(d).wait_recv()

    squares = lax.fori_loop(0, n, lambda i, s: s + squares_all[i], jnp.zeros((1, cols), jnp.float32))
    next_squares[0] = squares[:, : 2 * BLK]

    def to_core_squares():
        return pltpu.make_async_remote_copy(
            next_squares.at[0], next_squares.at[1], nsq_ss, nsq_rs,
            device_id={"snp": lax.rem(core + snps - 1, snps)})

    @pl.when(has_prev)
    def _():
        to_core_squares().start()

    own_scale = lax.rsqrt(squares + EPS)
    for b in range(blocks):
        scale[b] = own_scale[:, b * BLK:(b + 1) * BLK]
        for f in range(2):
            lanes = [own_scale[:, b * BLK + q * quarter:b * BLK + (q + 1) * quarter] for q in (2 * f, 2 * f + 1)]
            line = jnp.where(near == 0, lanes[0], lanes[1]) * UNIT
            row_scale[b, f * quarter:(f + 1) * quarter] = jnp.transpose(
                jnp.broadcast_to(line, (quarter, quarter)))

    @pl.when(has_next)
    def _():
        to_core_squares().wait_recv()
        nxt = lax.rsqrt(next_squares[1] + EPS)
        scale[blocks] = nxt[:, :BLK]
        scale[blocks + 1] = nxt[:, BLK:]
        to_core().wait_recv()

    def where(i):
        m, k = i // 3, i % 3
        b = m - k
        there = (b >= 0) & (b < blocks) & ((m < blocks) | has_next)
        return m, k, b, there

    def slot(k, b):
        return k * blocks + b

    def level_copy(level, t):
        v = (me // bits[level]) % 2
        return pltpu.make_async_remote_copy(
            level_send[level].at[t], level_recv[level].at[t], lev_ss.at[level, t], lev_rs.at[level, t],
            device_id={"smp": me + bits[level] * (1 - 2 * v)})

    def far_copy(t):
        return pltpu.make_async_remote_copy(
            far_send.at[t], far_recv.at[t], far_ss.at[t], far_rs.at[t], device_id={"smp": far_peer})

    def row0(level):
        lo = 0
        for j in range(level):
            lo = lo + ((me // bits[j]) % 2) * (quarter >> (j + 1))
        return lo

    def part(level):
        rows = quarter >> level
        return pl.ds(pl.multiple_of(row0(level), rows), rows)

    def send_level(level, t):
        rows = quarter >> (level + 1)
        v = (me // bits[level]) % 2
        start = pl.multiple_of(row0(level) + (1 - v) * rows, rows)
        level_send[level][t] = acc[t, :, pl.ds(start, rows), :].astype(WIRE)
        level_copy(level, t).start()

    def send_next(level, t):
        if level < len(bits):
            send_level(level, t)
        else:
            far_send[t] = acc[t, 1 - far, part(level), :].astype(WIRE)
            far_copy(t).start()

    def step(i):
        m, k, b, there = where(i)
        inside = i < 3 * (blocks + 2)

        @pl.when(inside & (k == 0))
        def _():
            @pl.when(m < blocks)
            def _():
                raw(pl.multiple_of(m, 1)).wait_recv()

                @pl.when(has_prev & (m < 2))
                def _():
                    forward(m).start()

            @pl.when((m >= blocks) & has_next)
            def _():
                forward(m - blocks).wait_recv()

        @pl.when(inside & there)
        def _():
            t = slot(k, b)
            lhs = jnp.concatenate(
                [full[:, pl.ds(pl.multiple_of(b * BLK + (near + 2 * f) * quarter, quarter), quarter)]
                 for f in range(2)], axis=1)
            rhs = full[:, pl.ds(pl.multiple_of(m * BLK, BLK), BLK)]
            gram = lax.dot_general(lhs, rhs, (((0,), (0,)), ((), ())), preferred_element_type=jnp.float32)
            rs = row_scale[b]
            gram = gram * jnp.concatenate([rs] * (BLK // quarter), axis=1) * scale[m]
            acc[t] = gram.reshape(2, quarter, BLK)
            send_next(0, t)

        @pl.when(inside & (b >= 0) & (b < blocks) & jnp.logical_not(there))
        def _():
            out_ref[k, b] = jnp.zeros(out_ref.shape[2:], jnp.float32)

        for level in range(len(bits)):
            j = i - LAG * (level + 1)
            _, k2, b2, there2 = where(jnp.maximum(j, 0))

            @pl.when((j >= 0) & (j < 3 * (blocks + 2)) & there2)
            def _(level=level, k2=k2, b2=b2):
                t = slot(k2, b2)
                level_copy(level, t).wait_recv()
                mine = part(level + 1)
                acc[t, :, mine, :] = acc[t, :, mine, :] + level_recv[level][t].astype(jnp.float32)
                send_next(level + 1, t)

        j = i - LAG * (len(bits) + 1)
        _, k3, b3, there3 = where(jnp.maximum(j, 0))

        @pl.when((j >= 0) & there3)
        def _():
            t = slot(k3, b3)
            far_copy(t).wait_recv()
            total = acc[t, far, part(len(bits)), :] + far_recv[t].astype(jnp.float32)
            out_ref[k3, b3] = total * (1.0 / UNIT)

    @pl.loop(0, 3 * (blocks + 2) + LAG * (len(bits) + 1))
    def _(i):
        step(i)

    @pl.loop(1, n)
    def _(d):
        send_squares(d).wait_send()

    for b in range(blocks):
        raw(b).wait_send()

    @pl.when(has_prev)
    def _():
        to_core().wait_send()
        to_core_squares().wait_send()
        forward(0).wait_send()
        forward(1).wait_send()

    @pl.loop(0, 3 * (blocks + 2))
    def _(i):
        _, k, b, there = where(i)

        @pl.when(there)
        def _():
            t = slot(k, b)
            for level in range(len(bits)):
                level_copy(level, t).wait_send()
            far_copy(t).wait_send()


def shards(n, snps, dosage):
    samples, cols = dosage.shape
    blocks = cols // BLK
    tiles = 3 * blocks
    rows = BLK // n
    quarter = BLK // 4
    levels = max(0, (n // 4).bit_length() - 1)
    vmem = pltpu.VMEM
    sizes = [(tiles, 2, quarter >> (j + 1), BLK) for j in range(levels)]
    dma = pltpu.SemaphoreType.DMA
    scratch = [
        vmem((2 * samples, cols + 2 * BLK), jnp.bfloat16),
        vmem((n, 1, cols), jnp.float32),
        vmem((blocks + 2, 1, BLK), jnp.float32),
        vmem((blocks, 2 * quarter, quarter), jnp.float32),
        vmem((tiles, 2, quarter, BLK), jnp.float32),
        [vmem(s, WIRE) for s in sizes],
        [vmem(s, WIRE) for s in sizes],
        vmem((tiles, rows, BLK), WIRE),
        vmem((tiles, rows, BLK), WIRE),
        vmem((2, 1, 2 * BLK), jnp.float32),
        dma, dma((blocks,)), dma((blocks,)), dma, dma, dma((2,)), dma((2,)),
        dma((n,)), dma((n,)), dma, dma,
        dma((levels, tiles)), dma((levels, tiles)), dma((tiles,)), dma((tiles,)),
    ]
    flops = 2 * tiles * BLK * BLK * samples
    return pl.pallas_call(
        functools.partial(kernel, n, snps),
        out_shape=jax.ShapeDtypeStruct((3, blocks, rows, BLK), jnp.float32),
        in_specs=[pl.BlockSpec(memory_space=pl.ANY)],
        out_specs=pl.BlockSpec(memory_space=pltpu.VMEM),
        scratch_shapes=scratch,
        compiler_params=pltpu.CompilerParams(
            collective_id=0, has_side_effects=True, vmem_limit_bytes=48 * 2**20),
        cost_estimate=pl.CostEstimate(flops=flops, bytes_accessed=4 * samples * cols, transcendentals=0),
    )(dosage)


def solution(mesh):
    return jax.shard_map(
        functools.partial(shards, mesh.shape["smp"], mesh.shape["snp"]),
        mesh=mesh,
        in_specs=(P("smp", ("seg", "snp")),),
        out_specs=P(None, ("seg", "snp"), "smp", None),
        check_vma=False,
    )
```

```python
import functools

import jax
import jax.numpy as jnp
from jax import lax
from jax.experimental import pallas as pl
from jax.experimental.pallas import tpu as pltpu
from jax.sharding import PartitionSpec as P

BLK = 512
EPS = 1e-06
WIRE = jnp.bfloat16
UNIT = 256.0
LAG = 3


def pack(v):
    v2 = v * v
    v4 = v2 * v2
    return (v * v2 * v4 * (v4 * v4)).astype(WIRE)


def unpack(y):
    y = y.astype(jnp.float32)
    size = jnp.abs(y)
    root = jnp.exp2(jnp.log2(jnp.maximum(size, 2.0**-126)) * (1.0 / 15.0))
    return jnp.where(size < 2.0**-126, 0.0, jnp.where(y < 0, -root, root))


def kernel(n, snps, x_ref, out_ref, full, squares_all, scale, row_scale, acc, level_send, level_recv,
           far_send, far_recv, next_squares, local_sem, raw_ss, raw_rs, core_ss, core_rs, fwd_ss, fwd_rs,
           sq_ss, sq_rs, nsq_ss, nsq_rs, lev_ss, lev_rs, far_ss, far_rs):
    samples, cols = x_ref.shape
    blocks = cols // BLK
    quarter = BLK // 4
    me = lax.axis_index("smp")
    core = lax.axis_index("snp")
    has_next = core < snps - 1
    has_prev = core > 0
    near_bit, far_bit = n // 4, n // 2
    near = (me // near_bit) % 2
    far = me // far_bit
    near_peer = me + near_bit * (1 - 2 * near)
    far_peer = me + far_bit * (1 - 2 * far)
    bits = []
    bit = n // 8
    while bit >= 1:
        bits.append(bit)
        bit //= 2
    tiles = 3 * blocks

    barrier = pltpu.get_barrier_semaphore()

    @pl.loop(1, n)
    def _(d):
        pl.semaphore_signal(barrier, inc=1, device_id={"smp": lax.rem(me + d, n)})

    @pl.when(has_next)
    def _():
        pl.semaphore_signal(barrier, inc=1, device_id={"snp": core + 1})

    @pl.when(has_prev)
    def _():
        pl.semaphore_signal(barrier, inc=1, device_id={"snp": core - 1})

    load = pltpu.make_async_copy(x_ref, full.at[pl.ds(0, samples), pl.ds(0, cols)], local_sem)
    load.start()
    pl.semaphore_wait(barrier, n - 1 + jnp.where(has_next, 1, 0) + jnp.where(has_prev, 1, 0))

    def raw(b):
        return pltpu.make_async_remote_copy(
            x_ref.at[:, pl.ds(b * BLK, BLK)],
            full.at[pl.ds(samples, samples), pl.ds(b * BLK, BLK)],
            raw_ss.at[b], raw_rs.at[b], device_id={"smp": near_peer})

    def to_core():
        return pltpu.make_async_remote_copy(
            x_ref.at[:, pl.ds(0, 2 * BLK)],
            full.at[pl.ds(0, samples), pl.ds(cols, 2 * BLK)],
            core_ss, core_rs, device_id={"snp": lax.rem(core + snps - 1, snps)})

    def forward(b):
        return pltpu.make_async_remote_copy(
            full.at[pl.ds(samples, samples), pl.ds(pl.multiple_of(b * BLK, BLK), BLK)],
            full.at[pl.ds(samples, samples), pl.ds(pl.multiple_of(cols + b * BLK, BLK), BLK)],
            fwd_ss.at[b], fwd_rs.at[b], device_id={"snp": lax.rem(core + snps - 1, snps)})

    raw(0).start()

    @pl.when(has_prev)
    def _():
        to_core().start()

    load.wait()
    for b in range(blocks):
        def add(r, total, b=b):
            piece = full[pl.ds(pl.multiple_of(r * 16, 16), 16), b * BLK:(b + 1) * BLK].astype(jnp.float32)
            return total + piece * piece
        total = lax.fori_loop(0, samples // 16, add, jnp.zeros((16, BLK), jnp.float32))
        squares_all[me, :, b * BLK:(b + 1) * BLK] = jnp.sum(total, axis=0, keepdims=True)

    def send_squares(d):
        peer = lax.rem(me + d, n)
        return pltpu.make_async_remote_copy(
            squares_all.at[me], squares_all.at[me], sq_ss.at[peer], sq_rs.at[me], device_id={"smp": peer})

    def recv_squares(d):
        peer = lax.rem(me + d, n)
        return pltpu.make_async_remote_copy(
            squares_all.at[peer], squares_all.at[peer], sq_ss.at[peer], sq_rs.at[peer], device_id={"smp": peer})

    @pl.loop(1, n)
    def _(d):
        send_squares(d).start()

    @pl.loop(1, n)
    def _(d):
        recv_squares(d).wait_recv()

    squares = lax.fori_loop(0, n, lambda i, s: s + squares_all[i], jnp.zeros((1, cols), jnp.float32))
    next_squares[0] = squares[:, : 2 * BLK]

    def to_core_squares():
        return pltpu.make_async_remote_copy(
            next_squares.at[0], next_squares.at[1], nsq_ss, nsq_rs,
            device_id={"snp": lax.rem(core + snps - 1, snps)})

    @pl.when(has_prev)
    def _():
        to_core_squares().start()

    own_scale = lax.rsqrt(squares + EPS)
    for b in range(blocks):
        scale[b] = own_scale[:, b * BLK:(b + 1) * BLK]
        for f in range(2):
            lanes = [own_scale[:, b * BLK + q * quarter:b * BLK + (q + 1) * quarter] for q in (2 * f, 2 * f + 1)]
            line = jnp.where(near == 0, lanes[0], lanes[1]) * UNIT
            row_scale[b, f * quarter:(f + 1) * quarter] = jnp.transpose(
                jnp.broadcast_to(line, (quarter, quarter)))

    @pl.when(has_next)
    def _():
        to_core_squares().wait_recv()
        nxt = lax.rsqrt(next_squares[1] + EPS)
        scale[blocks] = nxt[:, :BLK]
        scale[blocks + 1] = nxt[:, BLK:]
        to_core().wait_recv()

    def where(i):
        m, k = i // 3, i % 3
        b = m - k
        there = (b >= 0) & (b < blocks) & ((m < blocks) | has_next)
        return m, k, b, there

    def slot(k, b):
        return k * blocks + b

    def level_copy(level, t):
        v = (me // bits[level]) % 2
        return pltpu.make_async_remote_copy(
            level_send[level].at[t], level_recv[level].at[t], lev_ss.at[level, t], lev_rs.at[level, t],
            device_id={"smp": me + bits[level] * (1 - 2 * v)})

    def far_copy(t):
        return pltpu.make_async_remote_copy(
            far_send.at[t], far_recv.at[t], far_ss.at[t], far_rs.at[t], device_id={"smp": far_peer})

    def row0(level):
        lo = 0
        for j in range(level):
            lo = lo + ((me // bits[j]) % 2) * (quarter >> (j + 1))
        return lo

    def part(level):
        rows = quarter >> level
        return pl.ds(pl.multiple_of(row0(level), rows), rows)

    def send_level(level, t):
        rows = quarter >> (level + 1)
        v = (me // bits[level]) % 2
        start = pl.multiple_of(row0(level) + (1 - v) * rows, rows)
        level_send[level][t] = pack(acc[t, :, pl.ds(start, rows), :].reshape(2 * rows, BLK))
        level_copy(level, t).start()

    def send_next(level, t):
        if level < len(bits):
            send_level(level, t)
        else:
            theirs = acc[t, 1 - far, part(level), :]
            far_send[t] = pack(jnp.concatenate([theirs[:, :BLK // 2], theirs[:, BLK // 2:]], axis=0))
            far_copy(t).start()

    def step(i):
        m, k, b, there = where(i)
        inside = i < 3 * (blocks + 2)

        @pl.when(inside & (k == 0))
        def _():
            @pl.when(m < blocks)
            def _():
                raw(m).wait_recv()

                @pl.when(m + 1 < blocks)
                def _():
                    raw(m + 1).start()

                @pl.when(has_prev & (m < 2))
                def _():
                    forward(m).start()

            @pl.when((m >= blocks) & has_next)
            def _():
                forward(m - blocks).wait_recv()

        @pl.when(inside & there)
        def _():
            t = slot(k, b)
            lhs = jnp.concatenate(
                [full[:, pl.ds(pl.multiple_of(b * BLK + (near + 2 * f) * quarter, quarter), quarter)]
                 for f in range(2)], axis=1)
            rhs = full[:, pl.ds(pl.multiple_of(m * BLK, BLK), BLK)]
            gram = lax.dot_general(lhs, rhs, (((0,), (0,)), ((), ())), preferred_element_type=jnp.float32)
            rs = row_scale[b]
            gram = gram * jnp.concatenate([rs] * (BLK // quarter), axis=1) * scale[m]
            acc[t] = gram.reshape(2, quarter, BLK)
            send_next(0, t)

        @pl.when(inside & (b >= 0) & (b < blocks) & jnp.logical_not(there))
        def _():
            out_ref[k, b] = jnp.zeros(out_ref.shape[2:], jnp.float32)

        for level in range(len(bits)):
            j = i - LAG * (level + 1)
            _, k2, b2, there2 = where(jnp.maximum(j, 0))

            @pl.when((j >= 0) & (j < 3 * (blocks + 2)) & there2)
            def _(level=level, k2=k2, b2=b2):
                t = slot(k2, b2)
                level_copy(level, t).wait_recv()
                mine = part(level + 1)
                other = unpack(level_recv[level][t]).reshape(2, quarter >> (level + 1), BLK)
                acc[t, :, mine, :] = acc[t, :, mine, :] + other
                send_next(level + 1, t)

        j = i - LAG * (len(bits) + 1)
        _, k3, b3, there3 = where(jnp.maximum(j, 0))

        @pl.when((j >= 0) & there3)
        def _():
            t = slot(k3, b3)
            far_copy(t).wait_recv()
            other = unpack(far_recv[t])
            rows = BLK // n
            other = jnp.concatenate([other[:rows], other[rows:]], axis=1)
            total = acc[t, far, part(len(bits)), :] + other
            out_ref[k3, b3] = total * (1.0 / UNIT)

    @pl.loop(0, 3 * (blocks + 2) + LAG * (len(bits) + 1))
    def _(i):
        step(i)

    @pl.loop(1, n)
    def _(d):
        send_squares(d).wait_send()

    for b in range(blocks):
        raw(b).wait_send()

    @pl.when(has_prev)
    def _():
        to_core().wait_send()
        to_core_squares().wait_send()
        forward(0).wait_send()
        forward(1).wait_send()

    @pl.loop(0, 3 * (blocks + 2))
    def _(i):
        _, k, b, there = where(i)

        @pl.when(there)
        def _():
            t = slot(k, b)
            for level in range(len(bits)):
                level_copy(level, t).wait_send()
            far_copy(t).wait_send()


def shards(n, snps, dosage):
    samples, cols = dosage.shape
    blocks = cols // BLK
    tiles = 3 * blocks
    rows = BLK // n
    quarter = BLK // 4
    levels = max(0, (n // 4).bit_length() - 1)
    vmem = pltpu.VMEM
    sizes = [(tiles, quarter >> j, BLK) for j in range(levels)]
    dma = pltpu.SemaphoreType.DMA
    scratch = [
        vmem((2 * samples, cols + 2 * BLK), jnp.bfloat16),
        vmem((n, 1, cols), jnp.float32),
        vmem((blocks + 2, 1, BLK), jnp.float32),
        vmem((blocks, 2 * quarter, quarter), jnp.float32),
        vmem((tiles, 2, quarter, BLK), jnp.float32),
        [vmem(s, WIRE) for s in sizes],
        [vmem(s, WIRE) for s in sizes],
        vmem((tiles, 2 * rows, BLK // 2), WIRE),
        vmem((tiles, 2 * rows, BLK // 2), WIRE),
        vmem((2, 1, 2 * BLK), jnp.float32),
        dma, dma((blocks,)), dma((blocks,)), dma, dma, dma((2,)), dma((2,)),
        dma((n,)), dma((n,)), dma, dma,
        dma((levels, tiles)), dma((levels, tiles)), dma((tiles,)), dma((tiles,)),
    ]
    flops = 2 * tiles * BLK * BLK * samples
    return pl.pallas_call(
        functools.partial(kernel, n, snps),
        out_shape=jax.ShapeDtypeStruct((3, blocks, rows, BLK), jnp.float32),
        in_specs=[pl.BlockSpec(memory_space=pl.ANY)],
        out_specs=pl.BlockSpec(memory_space=pltpu.VMEM),
        scratch_shapes=scratch,
        compiler_params=pltpu.CompilerParams(
            collective_id=0, has_side_effects=True, vmem_limit_bytes=48 * 2**20),
        cost_estimate=pl.CostEstimate(flops=flops, bytes_accessed=4 * samples * cols, transcendentals=0),
    )(dosage)


def solution(mesh):
    return jax.shard_map(
        functools.partial(shards, mesh.shape["smp"], mesh.shape["snp"]),
        mesh=mesh,
        in_specs=(P("smp", ("seg", "snp")),),
        out_specs=P(None, ("seg", "snp"), "smp", None),
        check_vma=False,
    )
```

```python
import functools

import jax
import jax.numpy as jnp
from jax import lax
from jax.experimental import pallas as pl
from jax.experimental.pallas import tpu as pltpu
from jax.sharding import PartitionSpec as P

BLK = 512
EPS = 1e-06
WIRE = jnp.bfloat16
UNIT = 256.0
LAG = 3


def pack(v):
    v2 = v * v
    v4 = v2 * v2
    return (v * v2 * v4 * (v4 * v4)).astype(WIRE)


def unpack(y):
    y = y.astype(jnp.float32)
    size = jnp.abs(y)
    root = jnp.exp2(jnp.log2(jnp.maximum(size, 2.0**-126)) * (1.0 / 15.0))
    return jnp.where(size < 2.0**-126, 0.0, jnp.where(y < 0, -root, root))


def kernel(n, snps, x_ref, out_ref, full, squares_all, scale, row_scale, acc, level_send, level_recv,
           far_send, far_recv, next_squares, local_sem, raw_ss, raw_rs, core_ss, core_rs, fwd_ss, fwd_rs,
           sq_ss, sq_rs, nsq_ss, nsq_rs, lev_ss, lev_rs, far_ss, far_rs):
    samples, cols = x_ref.shape
    blocks = cols // BLK
    quarter = BLK // 4
    me = lax.axis_index("smp")
    core = lax.axis_index("snp")
    has_next = core < snps - 1
    has_prev = core > 0
    near_bit, far_bit = n // 4, n // 2
    near = (me // near_bit) % 2
    far = me // far_bit
    near_peer = me + near_bit * (1 - 2 * near)
    far_peer = me + far_bit * (1 - 2 * far)
    bits = []
    bit = n // 8
    while bit >= 1:
        bits.append(bit)
        bit //= 2
    tiles = 3 * blocks

    barrier = pltpu.get_barrier_semaphore()

    @pl.loop(1, n)
    def _(d):
        pl.semaphore_signal(barrier, inc=1, device_id={"smp": lax.rem(me + d, n)})

    @pl.when(has_next)
    def _():
        pl.semaphore_signal(barrier, inc=1, device_id={"snp": core + 1})

    @pl.when(has_prev)
    def _():
        pl.semaphore_signal(barrier, inc=1, device_id={"snp": core - 1})

    load = pltpu.make_async_copy(x_ref, full.at[pl.ds(0, samples), pl.ds(0, cols)], local_sem)
    load.start()
    pl.semaphore_wait(barrier, n - 1 + jnp.where(has_next, 1, 0) + jnp.where(has_prev, 1, 0))

    def arrival(m):
        return jnp.where(has_next, blocks - 1 - m, m)

    half = samples // 2

    def raw(j):
        b = pl.multiple_of(arrival(j // 2) * BLK, BLK)
        r = pl.multiple_of((j % 2) * half, half)
        return pltpu.make_async_remote_copy(
            x_ref.at[pl.ds(r, half), pl.ds(b, BLK)],
            full.at[pl.ds(pl.multiple_of(samples + r, half), half), pl.ds(b, BLK)],
            raw_ss.at[j], raw_rs.at[j], device_id={"smp": near_peer})

    def to_core():
        return pltpu.make_async_remote_copy(
            x_ref.at[:, pl.ds(0, 2 * BLK)],
            full.at[pl.ds(0, samples), pl.ds(cols, 2 * BLK)],
            core_ss, core_rs, device_id={"snp": lax.rem(core + snps - 1, snps)})

    def forward(b):
        return pltpu.make_async_remote_copy(
            full.at[pl.ds(samples, samples), pl.ds(pl.multiple_of(b * BLK, BLK), BLK)],
            full.at[pl.ds(samples, samples), pl.ds(pl.multiple_of(cols + b * BLK, BLK), BLK)],
            fwd_ss.at[b], fwd_rs.at[b], device_id={"snp": lax.rem(core + snps - 1, snps)})

    raw(0).start()
    raw(1).start()

    @pl.when(has_prev)
    def _():
        to_core().start()

    load.wait()
    for b in range(blocks):
        def add(r, total, b=b):
            piece = full[pl.ds(pl.multiple_of(r * 16, 16), 16), b * BLK:(b + 1) * BLK].astype(jnp.float32)
            return total + piece * piece
        total = lax.fori_loop(0, samples // 16, add, jnp.zeros((16, BLK), jnp.float32))
        squares_all[me, :, b * BLK:(b + 1) * BLK] = jnp.sum(total, axis=0, keepdims=True)

    def send_squares(d):
        peer = lax.rem(me + d, n)
        return pltpu.make_async_remote_copy(
            squares_all.at[me], squares_all.at[me], sq_ss.at[peer], sq_rs.at[me], device_id={"smp": peer})

    def recv_squares(d):
        peer = lax.rem(me + d, n)
        return pltpu.make_async_remote_copy(
            squares_all.at[peer], squares_all.at[peer], sq_ss.at[peer], sq_rs.at[peer], device_id={"smp": peer})

    @pl.loop(1, n)
    def _(d):
        send_squares(d).start()

    @pl.loop(1, n)
    def _(d):
        recv_squares(d).wait_recv()

    squares = lax.fori_loop(0, n, lambda i, s: s + squares_all[i], jnp.zeros((1, cols), jnp.float32))
    next_squares[0] = squares[:, : 2 * BLK]

    def to_core_squares():
        return pltpu.make_async_remote_copy(
            next_squares.at[0], next_squares.at[1], nsq_ss, nsq_rs,
            device_id={"snp": lax.rem(core + snps - 1, snps)})

    @pl.when(has_prev)
    def _():
        to_core_squares().start()

    own_scale = lax.rsqrt(squares + EPS)
    for b in range(blocks):
        scale[b] = own_scale[:, b * BLK:(b + 1) * BLK]
        for f in range(2):
            lanes = [own_scale[:, b * BLK + q * quarter:b * BLK + (q + 1) * quarter] for q in (2 * f, 2 * f + 1)]
            line = jnp.where(near == 0, lanes[0], lanes[1]) * UNIT
            row_scale[b, f * quarter:(f + 1) * quarter] = jnp.transpose(
                jnp.broadcast_to(line, (quarter, quarter)))

    @pl.when(has_next)
    def _():
        to_core_squares().wait_recv()
        nxt = lax.rsqrt(next_squares[1] + EPS)
        scale[blocks] = nxt[:, :BLK]
        scale[blocks + 1] = nxt[:, BLK:]
        to_core().wait_recv()

    @pl.when(jnp.logical_not(has_next))
    def _():
        for k in range(1, 3):
            for b in range(blocks - k, blocks):
                out_ref[k, b] = jnp.zeros(out_ref.shape[2:], jnp.float32)

    def where(i):
        m, k = i // 3, i % 3
        b = jnp.where(has_next, blocks - 1 - m, m - k)
        return m, k, b, b >= 0

    def slot(k, b):
        return k * blocks + b

    def level_copy(level, t):
        v = (me // bits[level]) % 2
        return pltpu.make_async_remote_copy(
            level_send[level].at[t], level_recv[level].at[t], lev_ss.at[level, t], lev_rs.at[level, t],
            device_id={"smp": me + bits[level] * (1 - 2 * v)})

    def far_copy(t):
        return pltpu.make_async_remote_copy(
            far_send.at[t], far_recv.at[t], far_ss.at[t], far_rs.at[t], device_id={"smp": far_peer})

    def row0(level):
        lo = 0
        for j in range(level):
            lo = lo + ((me // bits[j]) % 2) * (quarter >> (j + 1))
        return lo

    def part(level):
        rows = quarter >> level
        return pl.ds(pl.multiple_of(row0(level), rows), rows)

    def send_level(level, t):
        rows = quarter >> (level + 1)
        v = (me // bits[level]) % 2
        start = pl.multiple_of(row0(level) + (1 - v) * rows, rows)
        level_send[level][t] = pack(acc[t, :, pl.ds(start, rows), :].reshape(2 * rows, BLK))
        level_copy(level, t).start()

    def send_next(level, t):
        if level < len(bits):
            send_level(level, t)
        else:
            theirs = acc[t, 1 - far, part(level), :]
            far_send[t] = pack(jnp.concatenate([theirs[:, :BLK // 2], theirs[:, BLK // 2:]], axis=0))
            far_copy(t).start()

    def step(i):
        m, k, b, there = where(i)
        inside = i < tiles

        @pl.when(inside & (k == 0))
        def _():
            for h in range(2):
                raw(2 * m + h).wait_recv()

                @pl.when(m + 1 < blocks)
                def _():
                    raw(2 * m + 2 + h).start()

            @pl.when(has_prev & (arrival(m) < 2))
            def _():
                forward(arrival(m)).start()

        @pl.when(has_next & (m == 0) & (k >= 1))
        def _():
            forward(k - 1).wait_recv()

        @pl.when(inside & there)
        def _():
            t = slot(k, b)
            lhs = jnp.concatenate(
                [full[:, pl.ds(pl.multiple_of(b * BLK + (near + 2 * f) * quarter, quarter), quarter)]
                 for f in range(2)], axis=1)
            rhs = full[:, pl.ds(pl.multiple_of((b + k) * BLK, BLK), BLK)]
            gram = lax.dot_general(lhs, rhs, (((0,), (0,)), ((), ())), preferred_element_type=jnp.float32)
            rs = row_scale[b]
            gram = gram * jnp.concatenate([rs] * (BLK // quarter), axis=1) * scale[b + k]
            acc[t] = gram.reshape(2, quarter, BLK)
            send_next(0, t)

        for level in range(len(bits)):
            j = i - LAG * (level + 1)
            _, k2, b2, there2 = where(jnp.maximum(j, 0))

            @pl.when((j >= 0) & (j < tiles) & there2)
            def _(level=level, k2=k2, b2=b2):
                t = slot(k2, b2)
                level_copy(level, t).wait_recv()
                mine = part(level + 1)
                other = unpack(level_recv[level][t]).reshape(2, quarter >> (level + 1), BLK)
                acc[t, :, mine, :] = acc[t, :, mine, :] + other
                send_next(level + 1, t)

        j = i - LAG * (len(bits) + 1)
        _, k3, b3, there3 = where(jnp.maximum(j, 0))

        @pl.when((j >= 0) & there3)
        def _():
            t = slot(k3, b3)
            far_copy(t).wait_recv()
            other = unpack(far_recv[t])
            rows = BLK // n
            other = jnp.concatenate([other[:rows], other[rows:]], axis=1)
            total = acc[t, far, part(len(bits)), :] + other
            out_ref[k3, b3] = total * (1.0 / UNIT)

    @pl.loop(0, tiles + LAG * (len(bits) + 1))
    def _(i):
        step(i)

    @pl.loop(1, n)
    def _(d):
        send_squares(d).wait_send()

    for j in range(2 * blocks):
        raw(j).wait_send()

    @pl.when(has_prev)
    def _():
        to_core().wait_send()
        to_core_squares().wait_send()
        forward(0).wait_send()
        forward(1).wait_send()

    @pl.loop(0, tiles)
    def _(i):
        _, k, b, there = where(i)

        @pl.when(there)
        def _():
            t = slot(k, b)
            for level in range(len(bits)):
                level_copy(level, t).wait_send()
            far_copy(t).wait_send()


def shards(n, snps, dosage):
    samples, cols = dosage.shape
    blocks = cols // BLK
    tiles = 3 * blocks
    rows = BLK // n
    quarter = BLK // 4
    levels = max(0, (n // 4).bit_length() - 1)
    vmem = pltpu.VMEM
    sizes = [(tiles, quarter >> j, BLK) for j in range(levels)]
    dma = pltpu.SemaphoreType.DMA
    scratch = [
        vmem((2 * samples, cols + 2 * BLK), jnp.bfloat16),
        vmem((n, 1, cols), jnp.float32),
        vmem((blocks + 2, 1, BLK), jnp.float32),
        vmem((blocks, 2 * quarter, quarter), jnp.float32),
        vmem((tiles, 2, quarter, BLK), jnp.float32),
        [vmem(s, WIRE) for s in sizes],
        [vmem(s, WIRE) for s in sizes],
        vmem((tiles, 2 * rows, BLK // 2), WIRE),
        vmem((tiles, 2 * rows, BLK // 2), WIRE),
        vmem((2, 1, 2 * BLK), jnp.float32),
        dma, dma((2 * blocks,)), dma((2 * blocks,)), dma, dma, dma((2,)), dma((2,)),
        dma((n,)), dma((n,)), dma, dma,
        dma((levels, tiles)), dma((levels, tiles)), dma((tiles,)), dma((tiles,)),
    ]
    flops = 2 * tiles * BLK * BLK * samples
    return pl.pallas_call(
        functools.partial(kernel, n, snps),
        out_shape=jax.ShapeDtypeStruct((3, blocks, rows, BLK), jnp.float32),
        in_specs=[pl.BlockSpec(memory_space=pl.ANY)],
        out_specs=pl.BlockSpec(memory_space=pltpu.VMEM),
        scratch_shapes=scratch,
        compiler_params=pltpu.CompilerParams(
            collective_id=0, has_side_effects=True, vmem_limit_bytes=48 * 2**20),
        cost_estimate=pl.CostEstimate(flops=flops, bytes_accessed=4 * samples * cols, transcendentals=0),
    )(dosage)


def solution(mesh):
    return jax.shard_map(
        functools.partial(shards, mesh.shape["smp"], mesh.shape["snp"]),
        mesh=mesh,
        in_specs=(P("smp", ("seg", "snp")),),
        out_specs=P(None, ("seg", "snp"), "smp", None),
        check_vma=False,
    )
```

```python
import functools

import jax
import jax.numpy as jnp
from jax import lax
from jax.experimental import pallas as pl
from jax.experimental.pallas import tpu as pltpu
from jax.sharding import PartitionSpec as P

BLK = 512
EPS = 1e-06
WIRE = jnp.bfloat16
UNIT = 256.0
LAG = 2
FAR_LAG = 3


def pack(v):
    v2 = v * v
    v4 = v2 * v2
    return (v * v2 * v4 * (v4 * v4)).astype(WIRE)


def unpack(y):
    y = y.astype(jnp.float32)
    size = jnp.abs(y)
    root = jnp.exp2(jnp.log2(jnp.maximum(size, 2.0**-126)) * (1.0 / 15.0))
    return jnp.where(size < 2.0**-126, 0.0, jnp.where(y < 0, -root, root))


def kernel(n, snps, x_ref, out_ref, full, squares_all, scale, row_scale, acc, level_send, level_recv,
           far_send, far_recv, next_squares, local_sem, raw_ss, raw_rs, core_ss, core_rs, fwd_ss, fwd_rs,
           sq_ss, sq_rs, nsq_ss, nsq_rs, lev_ss, lev_rs, far_ss, far_rs):
    samples, cols = x_ref.shape
    blocks = cols // BLK
    quarter = BLK // 4
    me = lax.axis_index("smp")
    core = lax.axis_index("snp")
    has_next = core < snps - 1
    has_prev = core > 0
    near_bit, far_bit = n // 4, n // 2
    near = (me // near_bit) % 2
    far = me // far_bit
    near_peer = me + near_bit * (1 - 2 * near)
    far_peer = me + far_bit * (1 - 2 * far)
    bits = []
    bit = n // 8
    while bit >= 1:
        bits.append(bit)
        bit //= 2
    tiles = 3 * blocks

    barrier = pltpu.get_barrier_semaphore()

    @pl.loop(1, n)
    def _(d):
        pl.semaphore_signal(barrier, inc=1, device_id={"smp": lax.rem(me + d, n)})

    @pl.when(has_next)
    def _():
        pl.semaphore_signal(barrier, inc=1, device_id={"snp": core + 1})

    @pl.when(has_prev)
    def _():
        pl.semaphore_signal(barrier, inc=1, device_id={"snp": core - 1})

    load = pltpu.make_async_copy(x_ref, full.at[pl.ds(0, samples), pl.ds(0, cols)], local_sem)
    load.start()
    pl.semaphore_wait(barrier, n - 1 + jnp.where(has_next, 1, 0) + jnp.where(has_prev, 1, 0))

    def arrival(m):
        return jnp.where(has_next, blocks - 1 - m, m)

    half = samples // 2

    def raw(j):
        b = pl.multiple_of(arrival(j // 2) * BLK, BLK)
        r = pl.multiple_of((j % 2) * half, half)
        return pltpu.make_async_remote_copy(
            x_ref.at[pl.ds(r, half), pl.ds(b, BLK)],
            full.at[pl.ds(pl.multiple_of(samples + r, half), half), pl.ds(b, BLK)],
            raw_ss.at[j], raw_rs.at[j], device_id={"smp": near_peer})

    def to_core():
        return pltpu.make_async_remote_copy(
            x_ref.at[:, pl.ds(0, 2 * BLK)],
            full.at[pl.ds(0, samples), pl.ds(cols, 2 * BLK)],
            core_ss, core_rs, device_id={"snp": lax.rem(core + snps - 1, snps)})

    def forward(b):
        return pltpu.make_async_remote_copy(
            full.at[pl.ds(samples, samples), pl.ds(pl.multiple_of(b * BLK, BLK), BLK)],
            full.at[pl.ds(samples, samples), pl.ds(pl.multiple_of(cols + b * BLK, BLK), BLK)],
            fwd_ss.at[b], fwd_rs.at[b], device_id={"snp": lax.rem(core + snps - 1, snps)})

    raw(0).start()
    raw(1).start()

    @pl.when(has_prev)
    def _():
        to_core().start()

    load.wait()
    for b in range(blocks):
        def add(r, total, b=b):
            piece = full[pl.ds(pl.multiple_of(r * 16, 16), 16), b * BLK:(b + 1) * BLK].astype(jnp.float32)
            return total + piece * piece
        total = lax.fori_loop(0, samples // 16, add, jnp.zeros((16, BLK), jnp.float32))
        squares_all[me, :, b * BLK:(b + 1) * BLK] = jnp.sum(total, axis=0, keepdims=True)

    def send_squares(d):
        peer = lax.rem(me + d, n)
        return pltpu.make_async_remote_copy(
            squares_all.at[me], squares_all.at[me], sq_ss.at[peer], sq_rs.at[me], device_id={"smp": peer})

    def recv_squares(d):
        peer = lax.rem(me + d, n)
        return pltpu.make_async_remote_copy(
            squares_all.at[peer], squares_all.at[peer], sq_ss.at[peer], sq_rs.at[peer], device_id={"smp": peer})

    @pl.loop(1, n)
    def _(d):
        send_squares(d).start()

    @pl.loop(1, n)
    def _(d):
        recv_squares(d).wait_recv()

    squares = lax.fori_loop(0, n, lambda i, s: s + squares_all[i], jnp.zeros((1, cols), jnp.float32))
    next_squares[0] = squares[:, : 2 * BLK]

    def to_core_squares():
        return pltpu.make_async_remote_copy(
            next_squares.at[0], next_squares.at[1], nsq_ss, nsq_rs,
            device_id={"snp": lax.rem(core + snps - 1, snps)})

    @pl.when(has_prev)
    def _():
        to_core_squares().start()

    own_scale = lax.rsqrt(squares + EPS)
    for b in range(blocks):
        scale[b] = own_scale[:, b * BLK:(b + 1) * BLK]
        for f in range(2):
            lanes = [own_scale[:, b * BLK + q * quarter:b * BLK + (q + 1) * quarter] for q in (2 * f, 2 * f + 1)]
            line = jnp.where(near == 0, lanes[0], lanes[1]) * UNIT
            row_scale[b, f * quarter:(f + 1) * quarter] = jnp.transpose(
                jnp.broadcast_to(line, (quarter, quarter)))

    @pl.when(has_next)
    def _():
        to_core_squares().wait_recv()
        nxt = lax.rsqrt(next_squares[1] + EPS)
        scale[blocks] = nxt[:, :BLK]
        scale[blocks + 1] = nxt[:, BLK:]
        to_core().wait_recv()

    @pl.when(jnp.logical_not(has_next))
    def _():
        for k in range(1, 3):
            for b in range(blocks - k, blocks):
                out_ref[k, b] = jnp.zeros(out_ref.shape[2:], jnp.float32)

    def where(i):
        m, k = i // 3, i % 3
        b = jnp.where(has_next, blocks - 1 - m, m - k)
        return m, k, b, b >= 0

    def slot(k, b):
        return k * blocks + b

    def level_copy(level, t):
        v = (me // bits[level]) % 2
        return pltpu.make_async_remote_copy(
            level_send[level].at[t], level_recv[level].at[t], lev_ss.at[level, t], lev_rs.at[level, t],
            device_id={"smp": me + bits[level] * (1 - 2 * v)})

    def far_copy(t):
        return pltpu.make_async_remote_copy(
            far_send.at[t], far_recv.at[t], far_ss.at[t], far_rs.at[t], device_id={"smp": far_peer})

    def row0(level):
        lo = 0
        for j in range(level):
            lo = lo + ((me // bits[j]) % 2) * (quarter >> (j + 1))
        return lo

    def part(level):
        rows = quarter >> level
        return pl.ds(pl.multiple_of(row0(level), rows), rows)

    def send_level(level, t):
        rows = quarter >> (level + 1)
        v = (me // bits[level]) % 2
        start = pl.multiple_of(row0(level) + (1 - v) * rows, rows)
        level_send[level][t] = pack(acc[t, :, pl.ds(start, rows), :].reshape(2 * rows, BLK))
        level_copy(level, t).start()

    def send_next(level, t):
        if level < len(bits):
            send_level(level, t)
        else:
            theirs = acc[t, 1 - far, part(level), :]
            far_send[t] = pack(jnp.concatenate([theirs[:, :BLK // 2], theirs[:, BLK // 2:]], axis=0))
            far_copy(t).start()

    def step(i):
        m, k, b, there = where(i)
        inside = i < tiles

        @pl.when(inside & (k == 0))
        def _():
            for h in range(2):
                raw(2 * m + h).wait_recv()

                @pl.when(m + 1 < blocks)
                def _():
                    raw(2 * m + 2 + h).start()

            @pl.when(has_prev & (arrival(m) < 2))
            def _():
                forward(arrival(m)).start()

        @pl.when(has_next & (m == 0) & (k >= 1))
        def _():
            forward(k - 1).wait_recv()

        @pl.when(inside & there)
        def _():
            t = slot(k, b)
            lhs = jnp.concatenate(
                [full[:, pl.ds(pl.multiple_of(b * BLK + (near + 2 * f) * quarter, quarter), quarter)]
                 for f in range(2)], axis=1)
            rhs = full[:, pl.ds(pl.multiple_of((b + k) * BLK, BLK), BLK)]
            gram = lax.dot_general(lhs, rhs, (((0,), (0,)), ((), ())), preferred_element_type=jnp.float32)
            rs = row_scale[b]
            gram = gram * jnp.concatenate([rs] * (BLK // quarter), axis=1) * scale[b + k]
            acc[t] = gram.reshape(2, quarter, BLK)
            send_next(0, t)

        for level in range(len(bits)):
            j = i - LAG * (level + 1)
            _, k2, b2, there2 = where(jnp.maximum(j, 0))

            @pl.when((j >= 0) & (j < tiles) & there2)
            def _(level=level, k2=k2, b2=b2):
                t = slot(k2, b2)
                level_copy(level, t).wait_recv()
                mine = part(level + 1)
                other = unpack(level_recv[level][t]).reshape(2, quarter >> (level + 1), BLK)
                acc[t, :, mine, :] = acc[t, :, mine, :] + other
                send_next(level + 1, t)

        j = i - (LAG * len(bits) + FAR_LAG)
        _, k3, b3, there3 = where(jnp.maximum(j, 0))

        @pl.when((j >= 0) & there3)
        def _():
            t = slot(k3, b3)
            far_copy(t).wait_recv()
            other = unpack(far_recv[t])
            rows = BLK // n
            other = jnp.concatenate([other[:rows], other[rows:]], axis=1)
            total = acc[t, far, part(len(bits)), :] + other
            out_ref[k3, b3] = total * (1.0 / UNIT)

    @pl.loop(0, tiles + (LAG * len(bits) + FAR_LAG))
    def _(i):
        step(i)

    @pl.loop(1, n)
    def _(d):
        send_squares(d).wait_send()

    for j in range(2 * blocks):
        raw(j).wait_send()

    @pl.when(has_prev)
    def _():
        to_core().wait_send()
        to_core_squares().wait_send()
        forward(0).wait_send()
        forward(1).wait_send()

    @pl.loop(0, tiles)
    def _(i):
        _, k, b, there = where(i)

        @pl.when(there)
        def _():
            t = slot(k, b)
            for level in range(len(bits)):
                level_copy(level, t).wait_send()
            far_copy(t).wait_send()


def shards(n, snps, dosage):
    samples, cols = dosage.shape
    blocks = cols // BLK
    tiles = 3 * blocks
    rows = BLK // n
    quarter = BLK // 4
    levels = max(0, (n // 4).bit_length() - 1)
    vmem = pltpu.VMEM
    sizes = [(tiles, quarter >> j, BLK) for j in range(levels)]
    dma = pltpu.SemaphoreType.DMA
    scratch = [
        vmem((2 * samples, cols + 2 * BLK), jnp.bfloat16),
        vmem((n, 1, cols), jnp.float32),
        vmem((blocks + 2, 1, BLK), jnp.float32),
        vmem((blocks, 2 * quarter, quarter), jnp.float32),
        vmem((tiles, 2, quarter, BLK), jnp.float32),
        [vmem(s, WIRE) for s in sizes],
        [vmem(s, WIRE) for s in sizes],
        vmem((tiles, 2 * rows, BLK // 2), WIRE),
        vmem((tiles, 2 * rows, BLK // 2), WIRE),
        vmem((2, 1, 2 * BLK), jnp.float32),
        dma, dma((2 * blocks,)), dma((2 * blocks,)), dma, dma, dma((2,)), dma((2,)),
        dma((n,)), dma((n,)), dma, dma,
        dma((levels, tiles)), dma((levels, tiles)), dma((tiles,)), dma((tiles,)),
    ]
    flops = 2 * tiles * BLK * BLK * samples
    return pl.pallas_call(
        functools.partial(kernel, n, snps),
        out_shape=jax.ShapeDtypeStruct((3, blocks, rows, BLK), jnp.float32),
        in_specs=[pl.BlockSpec(memory_space=pl.ANY)],
        out_specs=pl.BlockSpec(memory_space=pltpu.VMEM),
        scratch_shapes=scratch,
        compiler_params=pltpu.CompilerParams(
            collective_id=0, has_side_effects=True, vmem_limit_bytes=48 * 2**20),
        cost_estimate=pl.CostEstimate(flops=flops, bytes_accessed=4 * samples * cols, transcendentals=0),
    )(dosage)


def solution(mesh):
    return jax.shard_map(
        functools.partial(shards, mesh.shape["smp"], mesh.shape["snp"]),
        mesh=mesh,
        in_specs=(P("smp", ("seg", "snp")),),
        out_specs=P(None, ("seg", "snp"), "smp", None),
        check_vma=False,
    )
```

```python
import functools

import jax
import jax.numpy as jnp
from jax import lax
from jax.experimental import pallas as pl
from jax.experimental.pallas import tpu as pltpu
from jax.sharding import PartitionSpec as P

BLK = 512
EPS = 1e-06
WIRE = jnp.bfloat16
UNIT = 256.0
LAG = 2
FAR_LAG = 3


def pack(v):
    v2 = v * v
    v4 = v2 * v2
    return (v * v2 * v4 * (v4 * v4)).astype(WIRE)


def unpack(y):
    y = y.astype(jnp.float32)
    size = jnp.abs(y)
    root = jnp.exp2(jnp.log2(jnp.maximum(size, 2.0**-126)) * (1.0 / 15.0))
    return jnp.where(size < 2.0**-126, 0.0, jnp.where(y < 0, -root, root))


def kernel(n, snps, x_ref, out_ref, full, squares_all, scale, row_scale, acc, level_send, level_recv,
           far_send, far_recv, next_squares, local_sem, raw_ss, raw_rs, core_ss, core_rs, fwd_ss, fwd_rs,
           sq_ss, sq_rs, nsq_ss, nsq_rs, lev_ss, lev_rs, far_ss, far_rs):
    samples, cols = x_ref.shape
    blocks = cols // BLK
    quarter = BLK // 4
    me = lax.axis_index("smp")
    core = lax.axis_index("snp")
    has_next = core < snps - 1
    has_prev = core > 0
    near_bit, far_bit = n // 4, n // 2
    near = (me // near_bit) % 2
    far = me // far_bit
    near_peer = me + near_bit * (1 - 2 * near)
    far_peer = me + far_bit * (1 - 2 * far)
    bits = []
    bit = n // 8
    while bit >= 1:
        bits.append(bit)
        bit //= 2
    tiles = 3 * blocks

    barrier = pltpu.get_barrier_semaphore()

    @pl.loop(1, n)
    def _(d):
        pl.semaphore_signal(barrier, inc=1, device_id={"smp": lax.rem(me + d, n)})

    @pl.when(has_next)
    def _():
        pl.semaphore_signal(barrier, inc=1, device_id={"snp": core + 1})

    @pl.when(has_prev)
    def _():
        pl.semaphore_signal(barrier, inc=1, device_id={"snp": core - 1})

    load = pltpu.make_async_copy(x_ref, full.at[pl.ds(0, samples), pl.ds(0, cols)], local_sem)
    load.start()
    pl.semaphore_wait(barrier, n - 1 + jnp.where(has_next, 1, 0) + jnp.where(has_prev, 1, 0))

    def arrival(m):
        return jnp.where(has_next, blocks - 1 - m, m)

    half = samples // 2

    def raw(j):
        b = pl.multiple_of(arrival(j // 2) * BLK, BLK)
        r = pl.multiple_of((j % 2) * half, half)
        return pltpu.make_async_remote_copy(
            x_ref.at[pl.ds(r, half), pl.ds(b, BLK)],
            full.at[pl.ds(pl.multiple_of(samples + r, half), half), pl.ds(b, BLK)],
            raw_ss.at[j], raw_rs.at[j], device_id={"smp": near_peer})

    def to_core():
        return pltpu.make_async_remote_copy(
            x_ref.at[:, pl.ds(0, 2 * BLK)],
            full.at[pl.ds(0, samples), pl.ds(cols, 2 * BLK)],
            core_ss, core_rs, device_id={"snp": lax.rem(core + snps - 1, snps)})

    def forward(b):
        return pltpu.make_async_remote_copy(
            full.at[pl.ds(samples, samples), pl.ds(pl.multiple_of(b * BLK, BLK), BLK)],
            full.at[pl.ds(samples, samples), pl.ds(pl.multiple_of(cols + b * BLK, BLK), BLK)],
            fwd_ss.at[b], fwd_rs.at[b], device_id={"snp": lax.rem(core + snps - 1, snps)})

    raw(0).start()
    raw(1).start()
    raw(2).start()

    @pl.when(has_prev)
    def _():
        to_core().start()

    load.wait()
    for b in range(blocks):
        def add(r, total, b=b):
            piece = full[pl.ds(pl.multiple_of(r * 16, 16), 16), b * BLK:(b + 1) * BLK].astype(jnp.float32)
            return total + piece * piece
        total = lax.fori_loop(0, samples // 16, add, jnp.zeros((16, BLK), jnp.float32))
        squares_all[me, :, b * BLK:(b + 1) * BLK] = jnp.sum(total, axis=0, keepdims=True)

    def send_squares(d):
        peer = lax.rem(me + d, n)
        return pltpu.make_async_remote_copy(
            squares_all.at[me], squares_all.at[me], sq_ss.at[peer], sq_rs.at[me], device_id={"smp": peer})

    def recv_squares(d):
        peer = lax.rem(me + d, n)
        return pltpu.make_async_remote_copy(
            squares_all.at[peer], squares_all.at[peer], sq_ss.at[peer], sq_rs.at[peer], device_id={"smp": peer})

    @pl.loop(1, n)
    def _(d):
        send_squares(d).start()

    @pl.loop(1, n)
    def _(d):
        recv_squares(d).wait_recv()

    squares = lax.fori_loop(0, n, lambda i, s: s + squares_all[i], jnp.zeros((1, cols), jnp.float32))
    next_squares[0] = squares[:, : 2 * BLK]

    def to_core_squares():
        return pltpu.make_async_remote_copy(
            next_squares.at[0], next_squares.at[1], nsq_ss, nsq_rs,
            device_id={"snp": lax.rem(core + snps - 1, snps)})

    @pl.when(has_prev)
    def _():
        to_core_squares().start()

    own_scale = lax.rsqrt(squares + EPS)
    for b in range(blocks):
        scale[b] = own_scale[:, b * BLK:(b + 1) * BLK]
        for f in range(2):
            lanes = [own_scale[:, b * BLK + q * quarter:b * BLK + (q + 1) * quarter] for q in (2 * f, 2 * f + 1)]
            line = jnp.where(near == 0, lanes[0], lanes[1]) * UNIT
            row_scale[b, f * quarter:(f + 1) * quarter] = jnp.transpose(
                jnp.broadcast_to(line, (quarter, quarter)))

    @pl.when(has_next)
    def _():
        to_core_squares().wait_recv()
        nxt = lax.rsqrt(next_squares[1] + EPS)
        scale[blocks] = nxt[:, :BLK]
        scale[blocks + 1] = nxt[:, BLK:]
        to_core().wait_recv()

    @pl.when(jnp.logical_not(has_next))
    def _():
        for k in range(1, 3):
            for b in range(blocks - k, blocks):
                out_ref[k, b] = jnp.zeros(out_ref.shape[2:], jnp.float32)

    def where(i):
        m, k = i // 3, i % 3
        b = jnp.where(has_next, blocks - 1 - m, m - k)
        return m, k, b, b >= 0

    def slot(k, b):
        return k * blocks + b

    def level_copy(level, t):
        v = (me // bits[level]) % 2
        return pltpu.make_async_remote_copy(
            level_send[level].at[t], level_recv[level].at[t], lev_ss.at[level, t], lev_rs.at[level, t],
            device_id={"smp": me + bits[level] * (1 - 2 * v)})

    def far_copy(t):
        return pltpu.make_async_remote_copy(
            far_send.at[t], far_recv.at[t], far_ss.at[t], far_rs.at[t], device_id={"smp": far_peer})

    def row0(level):
        lo = 0
        for j in range(level):
            lo = lo + ((me // bits[j]) % 2) * (quarter >> (j + 1))
        return lo

    def part(level):
        rows = quarter >> level
        return pl.ds(pl.multiple_of(row0(level), rows), rows)

    def send_level(level, t):
        rows = quarter >> (level + 1)
        v = (me // bits[level]) % 2
        start = pl.multiple_of(row0(level) + (1 - v) * rows, rows)
        level_send[level][t] = pack(acc[t, :, pl.ds(start, rows), :].reshape(2 * rows, BLK))
        level_copy(level, t).start()

    def send_next(level, t):
        if level < len(bits):
            send_level(level, t)
        else:
            theirs = acc[t, 1 - far, part(level), :]
            far_send[t] = pack(jnp.concatenate([theirs[:, :BLK // 2], theirs[:, BLK // 2:]], axis=0))
            far_copy(t).start()

    def step(i):
        m, k, b, there = where(i)
        inside = i < tiles

        @pl.when(inside & (k == 0))
        def _():
            for h in range(2):
                raw(2 * m + h).wait_recv()

                @pl.when(2 * m + h + 3 < 2 * blocks)
                def _():
                    raw(2 * m + h + 3).start()

            @pl.when(has_prev & (arrival(m) < 2))
            def _():
                forward(arrival(m)).start()

        @pl.when(has_next & (m == 0) & (k >= 1))
        def _():
            forward(k - 1).wait_recv()

        @pl.when(inside & there)
        def _():
            t = slot(k, b)
            lhs = jnp.concatenate(
                [full[:, pl.ds(pl.multiple_of(b * BLK + (near + 2 * f) * quarter, quarter), quarter)]
                 for f in range(2)], axis=1)
            rhs = full[:, pl.ds(pl.multiple_of((b + k) * BLK, BLK), BLK)]
            gram = lax.dot_general(lhs, rhs, (((0,), (0,)), ((), ())), preferred_element_type=jnp.float32)
            rs = row_scale[b]
            gram = gram * jnp.concatenate([rs] * (BLK // quarter), axis=1) * scale[b + k]
            acc[t] = gram.reshape(2, quarter, BLK)
            send_next(0, t)

        for level in range(len(bits)):
            j = i - LAG * (level + 1)
            _, k2, b2, there2 = where(jnp.maximum(j, 0))

            @pl.when((j >= 0) & (j < tiles) & there2)
            def _(level=level, k2=k2, b2=b2):
                t = slot(k2, b2)
                level_copy(level, t).wait_recv()
                mine = part(level + 1)
                other = unpack(level_recv[level][t]).reshape(2, quarter >> (level + 1), BLK)
                acc[t, :, mine, :] = acc[t, :, mine, :] + other
                send_next(level + 1, t)

        j = i - (LAG * len(bits) + FAR_LAG)
        _, k3, b3, there3 = where(jnp.maximum(j, 0))

        @pl.when((j >= 0) & there3)
        def _():
            t = slot(k3, b3)
            far_copy(t).wait_recv()
            other = unpack(far_recv[t])
            rows = BLK // n
            other = jnp.concatenate([other[:rows], other[rows:]], axis=1)
            total = acc[t, far, part(len(bits)), :] + other
            out_ref[k3, b3] = total * (1.0 / UNIT)

    @pl.loop(0, tiles + (LAG * len(bits) + FAR_LAG))
    def _(i):
        step(i)

    @pl.loop(1, n)
    def _(d):
        send_squares(d).wait_send()

    for j in range(2 * blocks):
        raw(j).wait_send()

    @pl.when(has_prev)
    def _():
        to_core().wait_send()
        to_core_squares().wait_send()
        forward(0).wait_send()
        forward(1).wait_send()

    @pl.loop(0, tiles)
    def _(i):
        _, k, b, there = where(i)

        @pl.when(there)
        def _():
            t = slot(k, b)
            for level in range(len(bits)):
                level_copy(level, t).wait_send()
            far_copy(t).wait_send()


def shards(n, snps, dosage):
    samples, cols = dosage.shape
    blocks = cols // BLK
    tiles = 3 * blocks
    rows = BLK // n
    quarter = BLK // 4
    levels = max(0, (n // 4).bit_length() - 1)
    vmem = pltpu.VMEM
    sizes = [(tiles, quarter >> j, BLK) for j in range(levels)]
    dma = pltpu.SemaphoreType.DMA
    scratch = [
        vmem((2 * samples, cols + 2 * BLK), jnp.bfloat16),
        vmem((n, 1, cols), jnp.float32),
        vmem((blocks + 2, 1, BLK), jnp.float32),
        vmem((blocks, 2 * quarter, quarter), jnp.float32),
        vmem((tiles, 2, quarter, BLK), jnp.float32),
        [vmem(s, WIRE) for s in sizes],
        [vmem(s, WIRE) for s in sizes],
        vmem((tiles, 2 * rows, BLK // 2), WIRE),
        vmem((tiles, 2 * rows, BLK // 2), WIRE),
        vmem((2, 1, 2 * BLK), jnp.float32),
        dma, dma((2 * blocks,)), dma((2 * blocks,)), dma, dma, dma((2,)), dma((2,)),
        dma((n,)), dma((n,)), dma, dma,
        dma((levels, tiles)), dma((levels, tiles)), dma((tiles,)), dma((tiles,)),
    ]
    flops = 2 * tiles * BLK * BLK * samples
    return pl.pallas_call(
        functools.partial(kernel, n, snps),
        out_shape=jax.ShapeDtypeStruct((3, blocks, rows, BLK), jnp.float32),
        in_specs=[pl.BlockSpec(memory_space=pl.ANY)],
        out_specs=pl.BlockSpec(memory_space=pltpu.VMEM),
        scratch_shapes=scratch,
        compiler_params=pltpu.CompilerParams(
            collective_id=0, has_side_effects=True, vmem_limit_bytes=48 * 2**20),
        cost_estimate=pl.CostEstimate(flops=flops, bytes_accessed=4 * samples * cols, transcendentals=0),
    )(dosage)


def solution(mesh):
    return jax.shard_map(
        functools.partial(shards, mesh.shape["smp"], mesh.shape["snp"]),
        mesh=mesh,
        in_specs=(P("smp", ("seg", "snp")),),
        out_specs=P(None, ("seg", "snp"), "smp", None),
        check_vma=False,
    )
```
